256 devices in a mesh: replica: 32 (over x, z_lo, core), fsdp: 8 (over y, z_hi).
Axes of the slice: x: 4, y: 4, z: 8 (z_hi: 2, z_lo: 4; z = z_hi * 4 + z_lo), core: 2. Of those that a mesh axis runs over, the one named last changes fastest.
Arguments:
- fp8_codes: int32 [32, 4096, 1024], P('replica', 'fsdp'), may hold values from 32 to 207, as said below
- block_scales: int32 [32, 8, 4096], P('replica', None, 'fsdp'), may hold values from 122 to 127
- outer_params: float32 [4096, 1024], P(('fsdp', 'replica')), may hold values from -6 to 6
- outer_momentum: float32 [4096, 1024], P(('fsdp', 'replica')), may hold values from -4 to 4
- activations: bfloat16 [131072, 4096], P(('replica', 'fsdp')), may hold values from -6 to 6
- norm_gain: bfloat16 [4096], replicated, may hold values from 0.099609375 to 1.8984375
- cotangent: bfloat16 [131072, 1024], P(('replica', 'fsdp')), may hold values from -6 to 6
Outputs:
- projected: bfloat16 [131072, 1024], P(('replica', 'fsdp'))
- input_grad: bfloat16 [131072, 4096], P(('replica', 'fsdp'))
- weight_grad: bfloat16 [32, 4096, 1024], P('replica', 'fsdp')
- params_next: float32 [4096, 1024], P(('fsdp', 'replica'))
- momentum_next: float32 [4096, 1024], P(('fsdp', 'replica'))
The draws below stay inside these ranges and needn't reach their ends.
Inputs may be any that keep to these rules, and one draw needn't show every extreme that they name: `fp8_codes`: e4m3 codes: c // 128 is the sign, (c % 128) // 8 the exponent field, c % 8 the mantissa field; exponent fields lie between 4 and 9.
All inputs are finite; a program needn't handle non-finite values.
Results may differ from the reference program's by a relative error of at most 0.018.
Values may be sent and summed in bfloat16 or wider, within the bound.
A program may use at most 128 MiB of HBM per device.

```python
import jax
import jax.numpy as jnp
from jax import lax

D = 4096
TOK_DEV = 512
K = 1024
KB = 8
TOK_REP = 4096
ROWS = 131072
N_REPLICA = 32
N_FSDP = 8


def draw_fp8_codes(key, part):
    key = jax.random.fold_in(key, 11)
    key_sign, key_exponent, key_mantissa = jax.random.split(key, 3)
    extent = (N_REPLICA, D, K)
    negative = jax.random.randint(key_sign, extent, 0, 2)
    exponent = jax.random.randint(key_exponent, extent, 4, 10)
    mantissa = jax.random.randint(key_mantissa, extent, 0, 8)
    return (negative * 128 + exponent * 8 + mantissa).astype(jnp.int32)


def place_ends(array, rng, low, high):
    longest = array.shape.index(max(array.shape))
    spots = []
    for shift in (0, 1):
        where = [jax.random.randint(jax.random.fold_in(rng, axis), (), 0, length) for axis, length in enumerate(array.shape)]
        where[longest] = (where[longest] + shift) % array.shape[longest]
        spots.append(tuple(where))
    return array.at[spots[0]].set(low).at[spots[1]].set(high)


def steps_of(own_key, shape, cuts, smallest, largest):
    gain = 1.0
    for dim, shards_of in cuts:
        heights = jax.random.uniform(jax.random.fold_in(jax.random.fold_in(own_key, 6), dim), (shards_of,), jnp.float32, smallest / len(cuts), largest / len(cuts))
        gain = gain * jnp.repeat(jnp.exp(heights), shape[dim] // shards_of).reshape((-1,) + (1,) * (len(shape) - 1 - dim))
    return gain


def centred(rng, shape, spread, limit, shards=(), held_as=jnp.bfloat16):
    values = spread * jax.random.normal(rng, shape, jnp.float32)
    if shards:
        values = values * steps_of(rng, shape, shards, -0.22, 0.18)
    return jnp.clip(values, -limit, limit).astype(held_as)


def setup_inputs(seed: int = 0) -> dict:
    arg_keys = jax.random.split(jax.random.key(seed), 8)
    return {
        "fp8_codes": draw_fp8_codes(jax.random.fold_in(arg_keys[7], 71), 0),
        "block_scales": place_ends(jax.random.randint(arg_keys[1], (N_REPLICA, KB, D), 122, 128), jax.random.fold_in(arg_keys[1], 1), 122, 127).astype(jnp.int32),
        "outer_params": centred(arg_keys[2], (D, K), 1.0, 6.0, ((0, 256),), jnp.float32),
        "outer_momentum": centred(arg_keys[3], (D, K), 0.3, 4.0, ((0, 256),), jnp.float32),
        "activations": centred(arg_keys[4], (ROWS, D), 1.0, 6.0, ((0, 256),)),
        "norm_gain": jnp.clip(1.0 + 0.18 * jax.random.normal(arg_keys[5], (D,), jnp.float32), 0.099609375, 1.8984375).astype(jnp.bfloat16),
        "cotangent": centred(arg_keys[6], (ROWS, K), 1.0, 6.0, ((0, 256),)),
    }


outer_rate = 0.7
outer_beta = 0.9
epsilon = 1e-05

def decode(code_block, scale_block):
    negative = code_block // 128
    exponent = code_block % 128 // 8
    mantissa = (code_block % 8).astype(jnp.float32)
    normal_value = (1.0 + mantissa / 8.0) * jnp.exp2((exponent - 7).astype(jnp.float32))
    small_value = mantissa / 8.0 * 0.015625
    magnitude = jnp.where(exponent > 0, normal_value, small_value)
    signed = jnp.where(negative > 0, -magnitude, magnitude)
    factor = jnp.exp2((scale_block - 127).astype(jnp.float32))
    row_count = code_block.shape[0]
    blocks = factor.shape[0]
    shaped = signed.reshape(row_count, blocks, code_block.shape[1] // blocks)
    return (shaped * jnp.transpose(factor)[:, :, None]).reshape(code_block.shape)

def reference(fp8_codes, block_scales, outer_params, outer_momentum, activations, norm_gain, cotangent):

    def accumulate(running, pair):
        return (running + decode(pair[0], pair[1]), None)
    total, _ = lax.scan(accumulate, jnp.zeros((D, K), jnp.float32), (fp8_codes, block_scales))
    delta = total / N_REPLICA
    momentum_next = outer_beta * outer_momentum + delta
    params_next = outer_params - outer_rate * (delta + outer_beta * momentum_next)
    weight = params_next.astype(jnp.bfloat16)
    factor = D ** (-0.5)
    gain_wide = norm_gain.astype(jnp.float32)

    def replica_pass(inputs):
        token_rows, upstream = inputs
        wide_rows = token_rows.astype(jnp.float32)
        inverse = lax.rsqrt(lax.optimization_barrier(jnp.mean(wide_rows * wide_rows, axis=-1, keepdims=True)) + epsilon)
        unit = wide_rows * inverse
        normed = (unit * gain_wide).astype(jnp.bfloat16)
        projected = (jnp.dot(normed, weight, preferred_element_type=jnp.float32) * factor).astype(jnp.bfloat16)
        back = jnp.dot(upstream, weight.T, preferred_element_type=jnp.float32) * factor * gain_wide
        input_grad = (inverse * (back - unit * lax.optimization_barrier(jnp.mean(back * unit, axis=-1, keepdims=True)))).astype(jnp.bfloat16)
        groups = normed.reshape(N_FSDP, TOK_DEV, D).astype(jnp.float32)
        up_groups = upstream.reshape(N_FSDP, TOK_DEV, K).astype(jnp.float32)
        partial_terms = (jnp.einsum('ftd,ftk->fdk', groups, up_groups) * factor).astype(jnp.bfloat16)
        partial_terms = lax.optimization_barrier(partial_terms)
        weight_grad = lax.optimization_barrier(jnp.sum(partial_terms.astype(jnp.float32), axis=0)).astype(jnp.bfloat16)
        return (projected, input_grad, weight_grad)
    projected, input_grad, weight_grad = lax.map(replica_pass, (activations.reshape(N_REPLICA, TOK_REP, D), cotangent.reshape(N_REPLICA, TOK_REP, K)))
    return (projected.reshape(ROWS, K), input_grad.reshape(ROWS, D), weight_grad, params_next, momentum_next)
```

```python
import functools

import jax
import jax.numpy as jnp
from jax import lax
from jax.experimental import pallas as pl
from jax.experimental.pallas import tpu as pltpu
from jax.sharding import PartitionSpec as P

outer_rate = 0.7
outer_beta = 0.9
epsilon = 1e-05
BF = jnp.bfloat16
F32 = jnp.float32
MESH = pl.DeviceIdType.MESH
D = 4096
T = 512
K = 1024
FACTOR = D ** (-0.5)


def device(x, y, z, c):
    return ((x * 4 + lax.rem(z, 4)) * 2 + c, y * 2 + lax.div(z, 4))


def kernel(
    codes, scales, params, moment, act, gain, cot,
    proj_o, ig_o, wg_o, pn_o, mn_o,
    codes_v, act_v, cot_v, nrm, inv_v, dec, g1r, g1s, g2r, g2s, g3r, wfull, acc, back,
    rb, ra, ps, own, pr, zs, zr, wgo, prj, mrow,
    lsem, osem, bsem, asem, psem, zsem, gsem, g2sem, g3sem, ysem, agsem, sbsem,
    bss, ass, pss, zss, gss, g2ss, g3ss, yss, zrs, xs, sbs,
):
    r = lax.axis_index("replica")
    f = lax.axis_index("fsdp")
    x, zl, c = lax.div(r, 8), lax.rem(lax.div(r, 2), 4), lax.rem(r, 2)
    y, zh = lax.div(f, 2), lax.rem(f, 2)
    z = zh * 4 + zl
    other = 1 - c
    swap = y + 1 - 2 * lax.rem(y, 2)
    p1 = c * (3 - y) + other * swap
    p2 = c * swap + other * (3 - y)
    q = lax.rem(y + 2, 4)
    sibling = device(x, y, z, other)
    dev_p1, dev_p2 = device(x, p1, z, c), device(x, p2, z, c)
    dev_z4 = device(x, y, lax.rem(z + 4, 8), c)
    xp = [lax.rem(x + d, 4) for d in (1, 2, 3)]
    zlp = [lax.rem(zl + d, 4) for d in (1, 2, 3)]
    yp = [lax.rem(y + d, 4) for d in (1, 2, 3)]
    zup, zdn = lax.rem(z + 1, 8), lax.rem(z + 7, 8)
    dev_zup, dev_zdn = device(x, y, zup, c), device(x, y, zdn, c)
    dev_x = [device(v, y, z, c) for v in xp]
    dev_zl = [device(x, y, zh * 4 + v, c) for v in zlp]
    dev_y = [device(x, v, z, c) for v in yp]

    started = []

    def send(src, dst, ss, rs, to):
        cp = pltpu.make_async_remote_copy(
            src_ref=src, dst_ref=dst, send_sem=ss, recv_sem=rs, device_id=to, device_id_type=MESH
        )
        cp.start()
        started.append(cp)

    def arrived(dst, rs):
        pltpu.make_async_remote_copy(
            src_ref=dst, dst_ref=dst, send_sem=bss, recv_sem=rs, device_id=sibling, device_id_type=MESH
        ).wait_recv()

    load_codes = pltpu.make_async_copy(codes.at[0], codes_v, lsem.at[0])
    load_act = pltpu.make_async_copy(act, act_v, lsem.at[1])
    load_cot = pltpu.make_async_copy(cot, cot_v, lsem.at[2])
    load_codes.start()
    load_act.start()
    load_cot.start()

    barrier = pltpu.get_barrier_semaphore()
    friends = [sibling, dev_z4, dev_zup, dev_zdn, *dev_x, *dev_zl, *dev_y]
    for to in friends:
        pl.semaphore_signal(barrier, inc=1, device_id=to, device_id_type=MESH)
    pl.semaphore_wait(barrier, len(friends))

    send(cot, rb, bss, bsem, dev_p1)

    factors = jnp.exp2((scales[0] - 127).astype(F32)).astype(BF)
    spread = (
        lax.broadcasted_iota(jnp.int32, (8, K), 1) // 128 == lax.broadcasted_iota(jnp.int32, (8, K), 0)
    ).astype(F32).astype(BF)
    acc[...] = lax.dot_general(factors, spread, (((0,), (0,)), ((), ())), preferred_element_type=F32)
    load_codes.wait()

    def decode_half(which):
        def step(g, _):
            rows = pl.ds(pl.multiple_of(g * 32 + which * 16, 16), 16)
            code = codes_v[rows, :]
            field = (code >> 3) & 15
            low = code & 7
            whole = jnp.where(field > 0, low + 8, low * 2) << field
            value = whole.astype(F32) * (acc[rows, :] * (2.0**-10))
            dec[which, g] = jnp.where(code >= 128, -value, value).astype(BF)
            return 0

        lax.fori_loop(0, 16, step, 0)

    decode_half(other)
    send(dec.at[other], g1r, gss, gsem, sibling)
    decode_half(c)
    arrived(g1r, gsem)

    def sum_one(g, _):
        g1s[g] = (dec[c, g].astype(F32) + g1r[g].astype(F32)).astype(BF)
        return 0

    lax.fori_loop(0, 16, sum_one, 0)
    for i in range(3):
        send(g1s.at[pl.ds(xp[i] * 4, 4)], g2r.at[i], g2ss.at[i], g2sem.at[i], dev_x[i])

    load_act.wait()
    gain_row = gain[...].astype(F32)

    def norm(t, _):
        rows = pl.ds(pl.multiple_of(t * 32, 32), 32)
        total = jnp.zeros((32, 128), F32)
        for j in range(32):
            a = act_v[rows, j * 128 : (j + 1) * 128].astype(F32)
            total = total + a * a
        inverse = lax.rsqrt(jnp.sum(total, axis=-1, keepdims=True) / D + epsilon)
        wide = jnp.broadcast_to(inverse, (32, 128))
        inv_v[rows, :] = wide
        for j in range(32):
            a = act_v[rows, j * 128 : (j + 1) * 128].astype(F32)
            nrm[j, rows, :] = (a * wide * gain_row[:, j * 128 : (j + 1) * 128]).astype(BF)
        return 0

    lax.fori_loop(0, 16, norm, 0)
    load_cot.wait()

    halves = (1 - zh, zh)

    def block(quarter, i, s):
        return quarter * 8 + halves[i] * 4 + s * 2

    def send_a(n):
        i, s, t = n // 4, (n // 2) % 2, n % 2
        quarter = q if t == 0 else p1
        send(nrm.at[pl.ds(block(quarter, i, s), 2)], ra.at[n], ass.at[n], asem.at[n], dev_p1)

    for n in range(8):
        send_a(n)

    def product(n):
        i, s, t = n // 4, (n // 2) % 2, n % 2
        j = block(p2 if t == 0 else y, i, s)
        arrived(ra.at[n], asem.at[n])
        mine = jnp.concatenate([nrm[j], nrm[j + 1]], axis=1)
        theirs = jnp.concatenate([ra[n, 0], ra[n, 1]], axis=1)
        dims = (((0,), (0,)), ((), ()))
        total = lax.dot_general(mine, cot_v[...], dims, preferred_element_type=F32)
        total = total + lax.dot_general(theirs, rb[...], dims, preferred_element_type=F32)
        total = total * FACTOR
        if t == 0:
            ps[n // 2] = total.astype(BF)
            send(ps.at[n // 2], pr.at[n // 2], pss.at[n // 2], psem.at[n // 2], dev_p2)
        else:
            own[n // 2] = total

    def reduce_y(m):
        arrived(pr.at[m], psem.at[m])
        total = own[m] + pr[m].astype(F32)
        if m < 2:
            zs[m] = total.astype(BF)
            send(zs.at[m], zr.at[m], zss.at[m], zsem.at[m], dev_z4)
        else:
            own[m] = total

    out_copies = []

    def reduce_z(m):
        arrived(zr.at[m], zsem.at[m])
        wgo[m * 256 : (m + 1) * 256, :] = (own[2 + m] + zr[m].astype(F32)).astype(BF)
        cp = pltpu.make_async_copy(
            wgo.at[m * 256 : (m + 1) * 256], wg_o.at[0, m * 256 : (m + 1) * 256], osem.at[m]
        )
        cp.start()
        out_copies.append(cp)

    def grad_x():
        for i in range(3):
            arrived(g2r.at[i], g2sem.at[i])
        total = g1s[pl.ds(x * 4, 4)].astype(F32)
        for i in range(3):
            total = total + g2r[i].astype(F32)
        g2s[...] = total.astype(BF)
        for i in range(3):
            send(g2s.at[zlp[i]], g3r.at[i], g3ss.at[i], g3sem.at[i], dev_zl[i])

    def grad_z():
        for i in range(3):
            arrived(g3r.at[i], g3sem.at[i])
        total = g2s[zl].astype(F32)
        for i in range(3):
            total = total + g3r[i].astype(F32)
        delta = total / 32.0
        momentum_next = outer_beta * moment[...] + delta
        params_next = params[...] - outer_rate * (delta + outer_beta * momentum_next)
        mn_o[...] = momentum_next
        pn_o[...] = params_next
        wfull[y, zh, x, zl, c] = params_next.astype(BF)
        mine = wfull.at[y, zh, x, zl, c]
        for i in range(3):
            send(mine, mine, yss.at[i], ysem.at[i], dev_y[i])

    def wblock(vx, vz, core):
        return wfull.at[:, lax.div(vz, 4), vx, lax.rem(vz, 4), core]

    def got_z(k, sign):
        vz = lax.rem(z + 8 + sign * k, 8)
        ref = wblock(x, vz, c)
        if k > 0:
            arrived(ref, agsem.at[x, vz])
        if k == 0:
            send(ref, ref, zrs.at[0], agsem.at[x, vz], dev_zup)
            send(ref, ref, zrs.at[1], agsem.at[x, vz], dev_zdn)
        elif sign < 0 and k < 4:
            send(ref, ref, zrs.at[1 + k], agsem.at[x, vz], dev_zup)
        elif sign > 0 and k < 3:
            send(ref, ref, zrs.at[4 + k], agsem.at[x, vz], dev_zdn)
        send(ref, ref, xs.at[0, vz], agsem.at[x, vz], dev_x[0])
        send(ref, ref, xs.at[1, vz], agsem.at[x, vz], dev_x[2])
        send(ref, ref, sbs.at[x, vz], sbsem.at[x, vz], sibling)

    def got_x(d, k, sign):
        vz = lax.rem(z + 8 + sign * k, 8)
        vx = xp[d - 1]
        ref = wblock(vx, vz, c)
        arrived(ref, agsem.at[vx, vz])
        if d == 3 and k % 2 == 0:
            send(ref, ref, xs.at[2, vz], agsem.at[vx, vz], dev_x[0])
        if d == 1 and k % 2 == 1:
            send(ref, ref, xs.at[2, vz], agsem.at[vx, vz], dev_x[2])
        send(ref, ref, sbs.at[vx, vz], sbsem.at[vx, vz], sibling)

    group = {0: [(0, 1)], 1: [(1, -1), (1, 1)], 2: [(2, -1), (2, 1)], 3: [(3, -1), (3, 1)], 4: [(4, -1)]}

    def z_step(k):
        for kk, sign in group[k]:
            got_z(kk, sign)

    def x_step(k):
        for kk, sign in group[k]:
            got_x(1, kk, sign)
            got_x(3, kk, sign)

    def far_step(k):
        for kk, sign in group[k]:
            got_x(2, kk, sign)

    def gather_y():
        for i in range(3):
            ref = wfull.at[yp[2 - i], zh, x, zl, c]
            arrived(ref, ysem.at[i])

    def piece(d, vh, first):
        vx = lax.rem(x + d, 4)
        for vl in range(4):
            vz = vh * 4 + vl
            arrived(wblock(vx, vz, other), sbsem.at[vx, vz])
        w = wfull[:, vh, vx].reshape(512, K)
        lhs = jnp.concatenate([nrm[v * 8 + vh * 4 + vx] for v in range(4)], axis=1)
        part = jnp.dot(lhs, w, preferred_element_type=F32)
        acc[...] = part if first else acc[...] + part
        b = lax.dot_general(cot_v[...], w, (((1,), (1,)), ((), ())), preferred_element_type=F32)
        for v in range(4):
            back[v * 8 + vh * 4 + vx] = b[:, v * 128 : (v + 1) * 128]

    grad_x()
    arrived(rb, bsem)
    product(0)
    grad_z()
    product(1)
    product(2)
    gather_y()
    z_step(0)
    product(3)
    z_step(1)
    reduce_y(0)
    product(4)
    z_step(2)
    reduce_y(1)
    product(5)
    product(6)
    z_step(3)
    product(7)
    z_step(4)
    x_step(0)
    x_step(1)
    far_step(0)
    x_step(2)
    far_step(1)
    piece(0, zh, True)
    x_step(3)
    far_step(2)
    piece(0, 1 - zh, False)
    x_step(4)
    far_step(3)
    far_step(4)
    reduce_y(2)
    reduce_y(3)
    for d in (1, 3, 2):
        piece(d, zh, False)
        piece(d, 1 - zh, False)

    def finish(t, _):
        rows = pl.ds(pl.multiple_of(t * 64, 64), 64)
        a = acc[rows, :]
        prj[rows, :] = (a * FACTOR).astype(BF)
        dots = jnp.sum(a * cot_v[rows, :].astype(F32), axis=-1, keepdims=True)
        mrow[rows, :] = jnp.broadcast_to(dots * (FACTOR / D), (64, 128))
        return 0

    lax.fori_loop(0, 8, finish, 0)
    cp = pltpu.make_async_copy(prj, proj_o, osem.at[2])
    cp.start()
    out_copies.append(cp)

    gain_scaled = gain_row * FACTOR

    def grad_in(t, _):
        rows = pl.ds(pl.multiple_of(t * 64, 64), 64)
        inverse = inv_v[rows, :]
        m = mrow[rows, :] * inverse * inverse
        for j in range(32):
            cols = slice(j * 128, (j + 1) * 128)
            a = act_v[rows, cols].astype(F32)
            out = back[j, rows, :] * gain_scaled[:, cols] * inverse - a * m
            act_v[rows, cols] = out.astype(BF)
        pltpu.make_async_copy(act_v.at[rows], ig_o.at[rows], osem.at[3 + t]).start()
        return 0

    lax.fori_loop(0, 8, grad_in, 0)
    reduce_z(0)
    reduce_z(1)

    for t in range(8):
        rows = slice(t * 64, (t + 1) * 64)
        pltpu.make_async_copy(act_v.at[rows], ig_o.at[rows], osem.at[3 + t]).wait()
    for cp in out_copies:
        cp.wait()
    for cp in started:
        cp.wait_send()


def shards(fp8_codes, block_scales, outer_params, outer_momentum, activations, norm_gain, cotangent):
    anywhere = pl.BlockSpec(memory_space=pl.ANY)
    vmem = pl.BlockSpec(memory_space=pltpu.VMEM)
    dma = pltpu.SemaphoreType.DMA
    return pl.pallas_call(
        kernel,
        name="diloco",
        out_shape=(
            jax.ShapeDtypeStruct((T, K), BF),
            jax.ShapeDtypeStruct((T, D), BF),
            jax.ShapeDtypeStruct((1, T, K), BF),
            jax.ShapeDtypeStruct((16, K), F32),
            jax.ShapeDtypeStruct((16, K), F32),
        ),
        in_specs=[anywhere, vmem, vmem, vmem, anywhere, vmem, anywhere],
        out_specs=(anywhere, anywhere, anywhere, vmem, vmem),
        scratch_shapes=[
            pltpu.VMEM((512, K), jnp.int32),
            pltpu.VMEM((T, D), BF),
            pltpu.VMEM((T, K), BF),
            pltpu.VMEM((32, T, 128), BF),
            pltpu.VMEM((T, 128), F32),
            pltpu.VMEM((2, 16, 16, K), BF),
            pltpu.VMEM((16, 16, K), BF),
            pltpu.VMEM((16, 16, K), BF),
            pltpu.VMEM((3, 4, 16, K), BF),
            pltpu.VMEM((4, 16, K), BF),
            pltpu.VMEM((3, 16, K), BF),
            pltpu.VMEM((4, 2, 4, 4, 2, 16, K), BF),
            pltpu.VMEM((T, K), F32),
            pltpu.VMEM((32, T, 128), F32),
            pltpu.VMEM((T, K), BF),
            pltpu.VMEM((8, 2, T, 128), BF),
            pltpu.VMEM((4, 256, K), BF),
            pltpu.VMEM((4, 256, K), F32),
            pltpu.VMEM((4, 256, K), BF),
            pltpu.VMEM((2, 256, K), BF),
            pltpu.VMEM((2, 256, K), BF),
            pltpu.VMEM((T, K), BF),
            pltpu.VMEM((T, K), BF),
            pltpu.VMEM((T, 128), F32),
            dma((3,)),
            dma((11,)),
            dma,
            dma((8,)),
            dma((4,)),
            dma((2,)),
            dma,
            dma((3,)),
            dma((3,)),
            dma((3,)),
            dma((4, 8)),
            dma((4, 8)),
            dma,
            dma((8,)),
            dma((4,)),
            dma((2,)),
            dma,
            dma((3,)),
            dma((3,)),
            dma((3,)),
            dma((7,)),
            dma((3, 8)),
            dma((4, 8)),
        ],
        compiler_params=pltpu.CompilerParams(
            collective_id=0, has_side_effects=True, vmem_limit_bytes=60 * 1024 * 1024
        ),
        cost_estimate=pl.CostEstimate(flops=13 * 10**9, bytes_accessed=14 * 2**20, transcendentals=0),
    )(
        fp8_codes, block_scales, outer_params, outer_momentum, activations,
        norm_gain.reshape(1, D), cotangent,
    )


def solution(mesh):
    in_specs = (
        P("replica", "fsdp", None),
        P("replica", None, "fsdp"),
        P(("fsdp", "replica"), None),
        P(("fsdp", "replica"), None),
        P(("replica", "fsdp"), None),
        P(),
        P(("replica", "fsdp"), None),
    )
    out_specs = (
        P(("replica", "fsdp"), None),
        P(("replica", "fsdp"), None),
        P("replica", "fsdp", None),
        P(("fsdp", "replica"), None),
        P(("fsdp", "replica"), None),
    )
    return jax.shard_map(shards, mesh=mesh, in_specs=in_specs, out_specs=out_specs, check_vma=False)
```

```python
import functools

import jax
import jax.numpy as jnp
from jax import lax
from jax.experimental import pallas as pl
from jax.experimental.pallas import tpu as pltpu
from jax.sharding import PartitionSpec as P

outer_rate = 0.7
outer_beta = 0.9
epsilon = 1e-05
BF = jnp.bfloat16
F32 = jnp.float32
MESH = pl.DeviceIdType.MESH
D = 4096
T = 512
K = 1024
FACTOR = D ** (-0.5)


def device(x, y, z, c):
    return ((x * 4 + lax.rem(z, 4)) * 2 + c, y * 2 + lax.div(z, 4))


def kernel(
    codes, scales, params, moment, act, gain, cot,
    act_v, back, prj, wgo, inv_v, mrow, pn_o, mn_o,
    codes_v, cot_v, nrm, dec, g1r, g1s, g2r, g2s, g3r, wfull, acc,
    rb, ra, ps, own, pr, zs, zr,
    lsem, bsem, asem, psem, zsem, gsem, g2sem, g3sem, zgsem, ygsem, xgsem, sbsem,
    bss, ass, pss, zss, gss, g2ss, g3ss, zgs, ygs, xgs, sbs,
):
    r = lax.axis_index("replica")
    f = lax.axis_index("fsdp")
    x, zl, c = lax.div(r, 8), lax.rem(lax.div(r, 2), 4), lax.rem(r, 2)
    y, zh = lax.div(f, 2), lax.rem(f, 2)
    z = zh * 4 + zl
    other = 1 - c
    swap = y + 1 - 2 * lax.rem(y, 2)
    p1 = c * (3 - y) + other * swap
    p2 = c * swap + other * (3 - y)
    q = lax.rem(y + 2, 4)
    sibling = device(x, y, z, other)
    dev_p1, dev_p2 = device(x, p1, z, c), device(x, p2, z, c)
    xp = [lax.rem(x + d, 4) for d in (1, 2, 3)]
    zlp = [lax.rem(zl + d, 4) for d in (1, 2, 3)]
    yp = [lax.rem(y + d, 4) for d in (1, 2, 3)]
    zp = [lax.rem(z + d, 8) for d in range(1, 8)]
    dev_x = [device(v, y, z, c) for v in xp]
    dev_zl = [device(x, y, zh * 4 + v, c) for v in zlp]
    dev_y = [device(x, v, z, c) for v in yp]
    dev_z = [device(x, y, v, c) for v in zp]
    dev_z4 = dev_z[3]

    started = []

    def send(src, dst, ss, rs, to):
        cp = pltpu.make_async_remote_copy(
            src_ref=src, dst_ref=dst, send_sem=ss, recv_sem=rs, device_id=to, device_id_type=MESH
        )
        cp.start()
        started.append(cp)

    def arrived(dst, rs):
        pltpu.make_async_remote_copy(
            src_ref=dst, dst_ref=dst, send_sem=bss, recv_sem=rs, device_id=sibling, device_id_type=MESH
        ).wait_recv()

    load_codes = pltpu.make_async_copy(codes.at[0], codes_v, lsem.at[0])
    load_act = pltpu.make_async_copy(act, act_v, lsem.at[1])
    load_cot = pltpu.make_async_copy(cot, cot_v, lsem.at[2])
    load_codes.start()
    load_act.start()
    load_cot.start()

    barrier = pltpu.get_barrier_semaphore()
    friends = [sibling, *dev_x, *dev_y, *dev_z]
    for to in friends:
        pl.semaphore_signal(barrier, inc=1, device_id=to, device_id_type=MESH)

    factors = jnp.exp2((scales[0] - 127).astype(F32)).astype(BF)
    spread = (
        lax.broadcasted_iota(jnp.int32, (8, K), 1) // 128 == lax.broadcasted_iota(jnp.int32, (8, K), 0)
    ).astype(F32).astype(BF)
    acc[...] = lax.dot_general(factors, spread, (((0,), (0,)), ((), ())), preferred_element_type=F32)
    load_codes.wait()

    def decode_half(which):
        def step(g, _):
            rows = pl.ds(pl.multiple_of(g * 32 + which * 16, 16), 16)
            code = codes_v[rows, :]
            field = (code >> 3) & 15
            low = code & 7
            whole = jnp.where(field > 0, low + 8, low * 2) << field
            value = whole.astype(F32) * (acc[rows, :] * (2.0**-10))
            dec[which, g] = jnp.where(code >= 128, -value, value).astype(BF)
            return 0

        lax.fori_loop(0, 16, step, 0)

    decode_half(other)
    pl.semaphore_wait(barrier, len(friends))
    send(cot, rb, bss, bsem, dev_p1)
    send(dec.at[other], g1r, gss, gsem, sibling)
    decode_half(c)
    arrived(g1r, gsem)

    def sum_one(g, _):
        g1s[g] = (dec[c, g].astype(F32) + g1r[g].astype(F32)).astype(BF)
        return 0

    lax.fori_loop(0, 16, sum_one, 0)
    for i in range(3):
        send(g1s.at[pl.ds(xp[i] * 4, 4)], g2r.at[i], g2ss.at[i], g2sem.at[i], dev_x[i])

    load_act.wait()
    gain_row = gain[...].astype(F32)

    def norm(t, _):
        rows = pl.ds(pl.multiple_of(t * 32, 32), 32)
        total = jnp.zeros((32, 128), F32)
        for j in range(32):
            a = act_v[rows, j * 128 : (j + 1) * 128].astype(F32)
            total = total + a * a
        inverse = lax.rsqrt(jnp.sum(total, axis=-1, keepdims=True) / D + epsilon)
        wide = jnp.broadcast_to(inverse, (32, 128))
        inv_v[rows, :] = wide
        for j in range(32):
            a = act_v[rows, j * 128 : (j + 1) * 128].astype(F32)
            nrm[j, rows, :] = (a * wide * gain_row[:, j * 128 : (j + 1) * 128]).astype(BF)
        return 0

    lax.fori_loop(0, 16, norm, 0)
    load_cot.wait()

    halves = (1 - zh, zh)
    chunks = ((0, 0, 1), (0, 1, 1), (0, 2, 2), (1, 0, 2), (1, 2, 2))

    def send_a(n):
        i, first, count = chunks[n // 2]
        quarter = (q, p1)[n % 2]
        src = nrm.at[pl.ds(quarter * 8 + halves[i] * 4 + first, count)]
        dst = ra.at[n % 2, i * 4 + first : i * 4 + first + count]
        send(src, dst, ass.at[n], asem.at[n], dev_p1)

    send_a(0)
    send_a(1)

    def product(n):
        m = n // 2
        i, first, count = chunks[m]
        low = i * 4 + first
        arrived(ra.at[n % 2, low : low + count], asem.at[n])
        if n < 8:
            send_a(n + 2)
        j = (p2, y)[n % 2] * 8 + halves[i] * 4 + first
        mine = jnp.concatenate([nrm[j + b] for b in range(count)], axis=1)
        theirs = jnp.concatenate([ra[n % 2, low + b] for b in range(count)], axis=1)
        dims = (((0,), (0,)), ((), ()))
        total = lax.dot_general(mine, cot_v[...], dims, preferred_element_type=F32)
        total = total + lax.dot_general(theirs, rb[...], dims, preferred_element_type=F32)
        total = total * FACTOR
        rows = slice(low * 128, (low + count) * 128)
        if n % 2 == 0:
            ps[rows, :] = total.astype(BF)
            send(ps.at[rows], pr.at[rows], pss.at[m], psem.at[m], dev_p2)
        else:
            own[rows, :] = total

    def reduce_y(m):
        i, first, count = chunks[m]
        rows = slice((i * 4 + first) * 128, (i * 4 + first + count) * 128)
        arrived(pr.at[rows], psem.at[m])
        total = own[rows, :] + pr[rows, :].astype(F32)
        if i == 0:
            zs[rows, :] = total.astype(BF)
            send(zs.at[rows], zr.at[rows], zss.at[m], zsem.at[m], dev_z4)
        else:
            own[rows, :] = total

    def reduce_z(m):
        _, first, count = chunks[m]
        rows = slice(first * 128, (first + count) * 128)
        arrived(zr.at[rows], zsem.at[m])
        summed = own[512 + first * 128 : 512 + (first + count) * 128, :]
        wgo[rows, :] = (summed + zr[rows, :].astype(F32)).astype(BF)

    def grad_x():
        for i in range(3):
            arrived(g2r.at[i], g2sem.at[i])
        total = g1s[pl.ds(x * 4, 4)].astype(F32)
        for i in range(3):
            total = total + g2r[i].astype(F32)
        g2s[...] = total.astype(BF)
        for i in range(3):
            send(g2s.at[zlp[i]], g3r.at[i], g3ss.at[i], g3sem.at[i], dev_zl[i])

    def grad_z():
        for i in range(3):
            arrived(g3r.at[i], g3sem.at[i])
        total = g2s[zl].astype(F32)
        for i in range(3):
            total = total + g3r[i].astype(F32)
        delta = total / 32.0
        momentum_next = outer_beta * moment[...] + delta
        params_next = params[...] - outer_rate * (delta + outer_beta * momentum_next)
        mn_o[...] = momentum_next
        pn_o[...] = params_next
        wfull[y, zh, x, zl, c] = params_next.astype(BF)
        mine = wfull.at[y, zh, x, zl, c]
        for i in range(7):
            send(mine, mine, zgs.at[i], zgsem.at[i], dev_z[i])

    def gather_z():
        for i in range(7):
            v = lax.rem(z + 7 - i, 8)
            arrived(wfull.at[y, lax.div(v, 4), x, lax.rem(v, 4), c], zgsem.at[i])

    def wblock(vx, vy, core):
        return wfull.at[vy, :, vx, :, core]

    def whalf(vx, vy, half):
        return wfull.at[vy, half, vx, :, c]

    def row_of(d):
        return lax.rem(y + d, 4)

    def y_step(d):
        vy = row_of(d)
        ref = wblock(x, vy, c)
        if d == 0:
            send(ref, ref, ygs.at[0], ygsem.at[vy, 0], dev_y[0])
            send(ref, ref, ygs.at[1], ygsem.at[vy, 0], dev_y[2])
        elif d == 3:
            arrived(ref, ygsem.at[vy, 0])
            send(whalf(x, vy, 0), whalf(x, vy, 0), ygs.at[2], ygsem.at[vy, 0], dev_y[0])
        elif d == 1:
            arrived(ref, ygsem.at[vy, 0])
            send(whalf(x, vy, 1), whalf(x, vy, 1), ygs.at[3], ygsem.at[vy, 1], dev_y[2])
        else:
            arrived(whalf(x, vy, 0), ygsem.at[vy, 0])
            arrived(whalf(x, vy, 1), ygsem.at[vy, 1])
        send(ref, ref, xgs.at[vy, 0], xgsem.at[x, vy, 0], dev_x[0])
        send(ref, ref, xgs.at[vy, 1], xgsem.at[x, vy, 0], dev_x[2])
        send(ref, ref, sbs.at[x, vy], sbsem.at[x, vy], sibling)

    def x_near(d):
        vy = row_of(d)
        for dx, half, to in ((3, 0, 0), (1, 1, 2)):
            vx = xp[dx - 1]
            ref = wblock(vx, vy, c)
            arrived(ref, xgsem.at[vx, vy, 0])
            part = whalf(vx, vy, half)
            send(part, part, xgs.at[vy, 2 + half], xgsem.at[vx, vy, half], dev_x[to])
            send(ref, ref, sbs.at[vx, vy], sbsem.at[vx, vy], sibling)

    def x_far(d):
        vy = row_of(d)
        vx = xp[1]
        for half in range(2):
            arrived(whalf(vx, vy, half), xgsem.at[vx, vy, half])
        ref = wblock(vx, vy, c)
        send(ref, ref, sbs.at[vx, vy], sbsem.at[vx, vy], sibling)

    def piece(dx, dy, first=False):
        vx, vy = lax.rem(x + dx, 4), row_of(dy)
        arrived(wblock(vx, vy, other), sbsem.at[vx, vy])
        w = wfull[vy, :, vx].reshape(256, K)
        j = vy * 8 + vx
        lhs = jnp.concatenate([nrm[j], nrm[j + 4]], axis=1)
        part = jnp.dot(lhs, w, preferred_element_type=F32)
        acc[...] = part if first else acc[...] + part
        b = lax.dot_general(cot_v[...], w, (((1,), (1,)), ((), ())), preferred_element_type=F32)
        back[j] = b[:, :128]
        back[j + 4] = b[:, 128:]

    grad_x()
    arrived(rb, bsem)
    product(0)
    product(1)
    grad_z()
    product(2)
    reduce_y(0)
    product(3)
    product(4)
    reduce_y(1)
    gather_z()
    y_step(0)
    product(5)
    piece(0, 0, True)
    x_near(0)
    reduce_y(2)
    product(6)
    y_step(3)
    y_step(1)
    product(7)
    x_far(0)
    piece(1, 0)
    piece(3, 0)
    x_near(3)
    reduce_y(3)
    x_near(1)
    product(8)
    y_step(2)
    piece(2, 0)
    piece(0, 3)
    piece(0, 1)
    product(9)
    x_far(3)
    x_far(1)
    for dy in (3, 1):
        piece(1, dy)
        piece(3, dy)
    x_near(2)
    piece(0, 2)
    piece(2, 3)
    piece(2, 1)
    x_far(2)
    reduce_y(4)
    piece(1, 2)
    piece(3, 2)
    piece(2, 2)

    def finish(t, _):
        rows = pl.ds(pl.multiple_of(t * 64, 64), 64)
        a = acc[rows, :]
        prj[rows, :] = (a * FACTOR).astype(BF)
        dots = jnp.sum(a * cot_v[rows, :].astype(F32), axis=-1, keepdims=True)
        mrow[rows, :] = jnp.broadcast_to(dots * (FACTOR / D), (64, 128))
        return 0

    lax.fori_loop(0, 8, finish, 0)
    for m in range(3):
        reduce_z(m)

    for cp in started:
        cp.wait_send()


def finish_kernel(act_v, back, prj, wgo, inv_v, mrow, gain, pn, mn, proj_o, ig_o, wg_o, pn_o, mn_o, grad, sem):
    copies = [
        pltpu.make_async_copy(prj, proj_o, sem.at[8]),
        pltpu.make_async_copy(wgo, wg_o.at[0], sem.at[9]),
        pltpu.make_async_copy(pn, pn_o, sem.at[10]),
        pltpu.make_async_copy(mn, mn_o, sem.at[11]),
    ]
    for cp in copies:
        cp.start()
    gain_scaled = gain[...].astype(F32) * FACTOR

    def grad_in(t, _):
        rows = pl.ds(pl.multiple_of(t * 64, 64), 64)
        inverse = inv_v[rows, :]
        m = mrow[rows, :] * inverse * inverse
        for j in range(32):
            cols = slice(j * 128, (j + 1) * 128)
            a = act_v[rows, cols].astype(F32)
            out = back[j, rows, :] * gain_scaled[:, cols] * inverse - a * m
            grad[rows, cols] = out.astype(BF)
        pltpu.make_async_copy(grad.at[rows], ig_o.at[rows], sem.at[t]).start()
        return 0

    lax.fori_loop(0, 8, grad_in, 0)
    for t in range(8):
        rows = slice(t * 64, (t + 1) * 64)
        pltpu.make_async_copy(grad.at[rows], ig_o.at[rows], sem.at[t]).wait()
    for cp in copies:
        cp.wait()


def shards(fp8_codes, block_scales, outer_params, outer_momentum, activations, norm_gain, cotangent):
    anywhere = pl.BlockSpec(memory_space=pl.ANY)
    vmem = pl.BlockSpec(memory_space=pltpu.VMEM)
    dma = pltpu.SemaphoreType.DMA
    gain_row = norm_gain.reshape(1, D)
    act_v, back, prj, wgo, inv_v, mrow, pn, mn = pl.pallas_call(
        kernel,
        name="exchange",
        out_shape=(
            pltpu.VMEM((T, D), BF),
            pltpu.VMEM((32, T, 128), F32),
            pltpu.VMEM((T, K), BF),
            pltpu.VMEM((T, K), BF),
            pltpu.VMEM((T, 128), F32),
            pltpu.VMEM((T, 128), F32),
            pltpu.VMEM((16, K), F32),
            pltpu.VMEM((16, K), F32),
        ),
        in_specs=[anywhere, vmem, vmem, vmem, anywhere, vmem, anywhere],
        out_specs=(vmem,) * 8,
        scratch_shapes=[
            pltpu.VMEM((512, K), jnp.int32),
            pltpu.VMEM((T, K), BF),
            pltpu.VMEM((32, T, 128), BF),
            pltpu.VMEM((2, 16, 16, K), BF),
            pltpu.VMEM((16, 16, K), BF),
            pltpu.VMEM((16, 16, K), BF),
            pltpu.VMEM((3, 4, 16, K), BF),
            pltpu.VMEM((4, 16, K), BF),
            pltpu.VMEM((3, 16, K), BF),
            pltpu.VMEM((4, 2, 4, 4, 2, 16, K), BF),
            pltpu.VMEM((T, K), F32),
            pltpu.VMEM((T, K), BF),
            pltpu.VMEM((2, 8, T, 128), BF),
            pltpu.VMEM((1024, K), BF),
            pltpu.VMEM((1024, K), F32),
            pltpu.VMEM((1024, K), BF),
            pltpu.VMEM((512, K), BF),
            pltpu.VMEM((512, K), BF),
            dma((3,)),
            dma,
            dma((10,)),
            dma((5,)),
            dma((3,)),
            dma,
            dma((3,)),
            dma((3,)),
            dma((7,)),
            dma((4, 2)),
            dma((4, 4, 2)),
            dma((4, 4)),
            dma,
            dma((10,)),
            dma((5,)),
            dma((3,)),
            dma,
            dma((3,)),
            dma((3,)),
            dma((7,)),
            dma((4,)),
            dma((4, 4)),
            dma((4, 4)),
        ],
        compiler_params=pltpu.CompilerParams(
            collective_id=0, has_side_effects=True, vmem_limit_bytes=45 * 1024 * 1024
        ),
        cost_estimate=pl.CostEstimate(flops=13 * 10**9, bytes_accessed=14 * 2**20, transcendentals=0),
    )(
        fp8_codes, block_scales, outer_params, outer_momentum, activations,
        gain_row, cotangent,
    )
    return pl.pallas_call(
        finish_kernel,
        name="finish",
        out_shape=(
            jax.ShapeDtypeStruct((T, K), BF),
            jax.ShapeDtypeStruct((T, D), BF),
            jax.ShapeDtypeStruct((1, T, K), BF),
            jax.ShapeDtypeStruct((16, K), F32),
            jax.ShapeDtypeStruct((16, K), F32),
        ),
        in_specs=[vmem] * 9,
        out_specs=(anywhere,) * 5,
        scratch_shapes=[pltpu.VMEM((T, D), BF), dma((12,))],
        compiler_params=pltpu.CompilerParams(vmem_limit_bytes=16 * 1024 * 1024),
    )(act_v, back, prj, wgo, inv_v, mrow, gain_row, pn, mn)


def solution(mesh):
    in_specs = (
        P("replica", "fsdp", None),
        P("replica", None, "fsdp"),
        P(("fsdp", "replica"), None),
        P(("fsdp", "replica"), None),
        P(("replica", "fsdp"), None),
        P(),
        P(("replica", "fsdp"), None),
    )
    out_specs = (
        P(("replica", "fsdp"), None),
        P(("replica", "fsdp"), None),
        P("replica", "fsdp", None),
        P(("fsdp", "replica"), None),
        P(("fsdp", "replica"), None),
    )
    return jax.shard_map(shards, mesh=mesh, in_specs=in_specs, out_specs=out_specs, check_vma=False)
```

```python
import functools

import jax
import jax.numpy as jnp
from jax import lax
from jax.experimental import pallas as pl
from jax.experimental.pallas import tpu as pltpu
from jax.sharding import PartitionSpec as P

outer_rate = 0.7
outer_beta = 0.9
epsilon = 1e-05
BF = jnp.bfloat16
F32 = jnp.float32
MESH = pl.DeviceIdType.MESH
D = 4096
T = 512
K = 1024
FACTOR = D ** (-0.5)


def device(x, y, z, c):
    return ((x * 4 + lax.rem(z, 4)) * 2 + c, y * 2 + lax.div(z, 4))


def kernel(
    codes, scales, params, moment, act, gain, cot,
    act_v, back, prj, wgo, inv_v, mrow, pn_o, mn_o,
    codes_v, cot_v, nrm, dec, g1r, g1s, g2r, g2s, g3r, wfull, acc,
    rb, ra, ps, own, pr, zs, zr,
    lsem, bsem, asem, psem, zsem, gsem, g2sem, g3sem, zgsem, ygsem, xgsem, sbsem,
    bss, ass, pss, zss, gss, g2ss, g3ss, zgs, ygs, xgs, sbs,
):
    r = lax.axis_index("replica")
    f = lax.axis_index("fsdp")
    x, zl, c = lax.div(r, 8), lax.rem(lax.div(r, 2), 4), lax.rem(r, 2)
    y, zh = lax.div(f, 2), lax.rem(f, 2)
    z = zh * 4 + zl
    other = 1 - c
    swap = y + 1 - 2 * lax.rem(y, 2)
    p1 = c * (3 - y) + other * swap
    p2 = c * swap + other * (3 - y)
    q = lax.rem(y + 2, 4)
    sibling = device(x, y, z, other)
    dev_p1, dev_p2 = device(x, p1, z, c), device(x, p2, z, c)
    xp = [lax.rem(x + d, 4) for d in (1, 2, 3)]
    zlp = [lax.rem(zl + d, 4) for d in (1, 2, 3)]
    yp = [lax.rem(y + d, 4) for d in (1, 2, 3)]
    zp = [lax.rem(z + d, 8) for d in range(1, 8)]
    dev_x = [device(v, y, z, c) for v in xp]
    dev_zl = [device(x, y, zh * 4 + v, c) for v in zlp]
    dev_y = [device(x, v, z, c) for v in yp]
    dev_z = [device(x, y, v, c) for v in zp]
    dev_z4 = dev_z[3]

    started = []

    def send(src, dst, ss, rs, to):
        cp = pltpu.make_async_remote_copy(
            src_ref=src, dst_ref=dst, send_sem=ss, recv_sem=rs, device_id=to, device_id_type=MESH
        )
        cp.start()
        started.append(cp)

    def arrived(dst, rs):
        pltpu.make_async_remote_copy(
            src_ref=dst, dst_ref=dst, send_sem=bss.at[0], recv_sem=rs, device_id=sibling, device_id_type=MESH
        ).wait_recv()

    load_codes = pltpu.make_async_copy(codes.at[0], codes_v, lsem.at[0])
    load_act = pltpu.make_async_copy(act, act_v, lsem.at[1])
    load_cot = pltpu.make_async_copy(cot, cot_v, lsem.at[2])
    load_codes.start()
    load_act.start()
    load_cot.start()

    barrier = pltpu.get_barrier_semaphore()
    friends = [sibling, *dev_x, *dev_y, *dev_z]
    for to in friends:
        pl.semaphore_signal(barrier, inc=1, device_id=to, device_id_type=MESH)
    pl.semaphore_wait(barrier, len(friends))

    def send_b(k):
        cols = slice(k * 512, (k + 1) * 512)
        send(cot.at[:, cols], rb.at[:, cols], bss.at[k], bsem.at[k], dev_p1)

    send_b(0)

    factors = jnp.exp2((scales[0] - 127).astype(F32)).astype(BF)
    spread = (
        lax.broadcasted_iota(jnp.int32, (8, K), 1) // 128 == lax.broadcasted_iota(jnp.int32, (8, K), 0)
    ).astype(F32).astype(BF)
    acc[...] = lax.dot_general(factors, spread, (((0,), (0,)), ((), ())), preferred_element_type=F32)
    load_codes.wait()

    def decode_half(which):
        def step(g, _):
            rows = pl.ds(pl.multiple_of(g * 32 + which * 16, 16), 16)
            code = codes_v[rows, :]
            field = (code >> 3) & 15
            low = code & 7
            whole = jnp.where(field > 0, low + 8, low * 2) << field
            value = whole.astype(F32) * (acc[rows, :] * (2.0**-10))
            dec[which, g] = jnp.where(code >= 128, -value, value).astype(BF)
            return 0

        lax.fori_loop(0, 16, step, 0)

    decode_half(other)
    send(dec.at[other], g1r, gss, gsem, sibling)
    decode_half(c)
    arrived(g1r, gsem)

    def sum_one(g, _):
        g1s[g] = (dec[c, g].astype(F32) + g1r[g].astype(F32)).astype(BF)
        return 0

    lax.fori_loop(0, 16, sum_one, 0)
    for i in range(3):
        send(g1s.at[pl.ds(xp[i] * 4, 4)], g2r.at[i], g2ss.at[i], g2sem.at[i], dev_x[i])

    load_act.wait()
    gain_row = gain[...].astype(F32).reshape(1, D)

    def norm(t, _):
        rows = pl.ds(pl.multiple_of(t * 32, 32), 32)
        total = jnp.zeros((32, 128), F32)
        for j in range(32):
            a = act_v[rows, j * 128 : (j + 1) * 128].astype(F32)
            total = total + a * a
        inverse = lax.rsqrt(jnp.sum(total, axis=-1, keepdims=True) / D + epsilon)
        wide = jnp.broadcast_to(inverse, (32, 128))
        inv_v[rows, :] = wide
        for j in range(32):
            a = act_v[rows, j * 128 : (j + 1) * 128].astype(F32)
            nrm[j, rows, :] = (a * wide * gain_row[:, j * 128 : (j + 1) * 128]).astype(BF)
        return 0

    lax.fori_loop(0, 16, norm, 0)
    load_cot.wait()

    halves = (1 - zh, zh)
    left, right, whole = slice(0, 512), slice(512, K), slice(0, K)
    chunks = (
        (0, 0, 1, left), (0, 1, 1, left), (0, 2, 2, left), (0, 0, 2, right), (0, 2, 2, right),
        (1, 0, 2, whole), (1, 2, 2, whole),
    )

    def send_a(m, t):
        i, first, count, _ = chunks[m]
        src = nrm.at[pl.ds((q, p1)[t] * 8 + halves[i] * 4 + first, count)]
        dst = ra.at[t, i * 4 + first : i * 4 + first + count]
        send(src, dst, ass.at[m, t], asem.at[m, t], dev_p1)

    send_a(0, 0)
    send_a(0, 1)

    def product(m, t):
        i, first, count, cols = chunks[m]
        low = i * 4 + first
        if m not in (3, 4):
            arrived(ra.at[t, low : low + count], asem.at[m, t])
        if m < 2:
            send_a(m + 1, t)
        if m == 3 and t == 0:
            arrived(rb.at[:, right], bsem.at[1])
        if m == 4:
            send_a(6, t)
        j = (p2, y)[t] * 8 + halves[i] * 4 + first
        mine = jnp.concatenate([nrm[j + b] for b in range(count)], axis=1)
        theirs = jnp.concatenate([ra[t, low + b] for b in range(count)], axis=1)
        dims = (((0,), (0,)), ((), ()))
        total = lax.dot_general(mine, cot_v[:, cols], dims, preferred_element_type=F32)
        total = total + lax.dot_general(theirs, rb[:, cols], dims, preferred_element_type=F32)
        total = total * FACTOR
        rows = slice(low * 128, (low + count) * 128)
        if t == 0:
            ps[rows, cols] = total.astype(BF)
            send(ps.at[rows, cols], pr.at[rows, cols], pss.at[m], psem.at[m], dev_p2)
        else:
            own[rows, cols] = total

    def reduce_y(m):
        i, first, count, cols = chunks[m]
        rows = slice((i * 4 + first) * 128, (i * 4 + first + count) * 128)
        arrived(pr.at[rows, cols], psem.at[m])
        total = own[rows, cols] + pr[rows, cols].astype(F32)
        if i == 0:
            zs[rows, cols] = total.astype(BF)
            send(zs.at[rows, cols], zr.at[rows, cols], zss.at[m], zsem.at[m], dev_z4)
        else:
            own[rows, cols] = total

    def reduce_z(m):
        _, first, count, cols = chunks[m]
        rows = slice(first * 128, (first + count) * 128)
        arrived(zr.at[rows, cols], zsem.at[m])
        summed = own[512 + first * 128 : 512 + (first + count) * 128, cols]
        wgo[rows, cols] = (summed + zr[rows, cols].astype(F32)).astype(BF)

    def grad_x():
        for i in range(3):
            arrived(g2r.at[i], g2sem.at[i])
        total = g1s[pl.ds(x * 4, 4)].astype(F32)
        for i in range(3):
            total = total + g2r[i].astype(F32)
        g2s[...] = total.astype(BF)
        for i in range(3):
            send(g2s.at[zlp[i]], g3r.at[i], g3ss.at[i], g3sem.at[i], dev_zl[i])

    def grad_z():
        for i in range(3):
            arrived(g3r.at[i], g3sem.at[i])
        total = g2s[zl].astype(F32)
        for i in range(3):
            total = total + g3r[i].astype(F32)
        delta = total / 32.0
        momentum_next = outer_beta * moment[...] + delta
        params_next = params[...] - outer_rate * (delta + outer_beta * momentum_next)
        mn_o[...] = momentum_next
        pn_o[...] = params_next
        wfull[y, zh, x, zl, c] = params_next.astype(BF)
        mine = wfull.at[y, zh, x, zl, c]
        for i in range(7):
            send(mine, mine, zgs.at[i], zgsem.at[i], dev_z[i])

    def gather_z():
        for i in range(7):
            v = lax.rem(z + 7 - i, 8)
            arrived(wfull.at[y, lax.div(v, 4), x, lax.rem(v, 4), c], zgsem.at[i])

    def wblock(vx, vy, core):
        return wfull.at[vy, :, vx, :, core]

    def whalf(vx, vy, half):
        return wfull.at[vy, half, vx, :, c]

    def row_of(d):
        return lax.rem(y + d, 4)

    def y_step(d):
        vy = row_of(d)
        ref = wblock(x, vy, c)
        if d == 0:
            send(ref, ref, ygs.at[0], ygsem.at[vy, 0], dev_y[0])
            send(ref, ref, ygs.at[1], ygsem.at[vy, 0], dev_y[2])
        elif d == 3:
            arrived(ref, ygsem.at[vy, 0])
            send(whalf(x, vy, 0), whalf(x, vy, 0), ygs.at[2], ygsem.at[vy, 0], dev_y[0])
        elif d == 1:
            arrived(ref, ygsem.at[vy, 0])
            send(whalf(x, vy, 1), whalf(x, vy, 1), ygs.at[3], ygsem.at[vy, 1], dev_y[2])
        else:
            arrived(whalf(x, vy, 0), ygsem.at[vy, 0])
            arrived(whalf(x, vy, 1), ygsem.at[vy, 1])
        send(ref, ref, xgs.at[vy, 0], xgsem.at[x, vy, 0], dev_x[0])
        send(ref, ref, xgs.at[vy, 1], xgsem.at[x, vy, 0], dev_x[2])
        send(ref, ref, sbs.at[x, vy], sbsem.at[x, vy], sibling)

    def x_near(d):
        vy = row_of(d)
        for dx, half, to in ((3, 0, 0), (1, 1, 2)):
            vx = xp[dx - 1]
            ref = wblock(vx, vy, c)
            arrived(ref, xgsem.at[vx, vy, 0])
            part = whalf(vx, vy, half)
            send(part, part, xgs.at[vy, 2 + half], xgsem.at[vx, vy, half], dev_x[to])
            send(ref, ref, sbs.at[vx, vy], sbsem.at[vx, vy], sibling)

    def x_far(d):
        vy = row_of(d)
        vx = xp[1]
        for half in range(2):
            arrived(whalf(vx, vy, half), xgsem.at[vx, vy, half])
        ref = wblock(vx, vy, c)
        send(ref, ref, sbs.at[vx, vy], sbsem.at[vx, vy], sibling)

    def piece(dx, dy, first=False):
        vx, vy = lax.rem(x + dx, 4), row_of(dy)
        arrived(wblock(vx, vy, other), sbsem.at[vx, vy])
        w = wfull[vy, :, vx].reshape(256, K)
        j = vy * 8 + vx
        lhs = jnp.concatenate([nrm[j], nrm[j + 4]], axis=1)
        part = jnp.dot(lhs, w, preferred_element_type=F32)
        acc[...] = part if first else acc[...] + part
        b = lax.dot_general(cot_v[...], w, (((1,), (1,)), ((), ())), preferred_element_type=F32)
        back[j] = b[:, :128]
        back[j + 4] = b[:, 128:]

    arrived(rb.at[:, left], bsem.at[0])
    product(0, 0)
    grad_x()
    product(0, 1)
    product(1, 0)
    product(1, 1)
    grad_z()
    product(2, 0)
    product(2, 1)
    gather_z()
    y_step(0)
    reduce_y(0)
    reduce_y(1)
    reduce_y(2)
    piece(0, 0, True)
    x_near(0)
    y_step(3)
    y_step(1)
    send_b(1)
    send_a(5, 0)
    send_a(5, 1)
    x_far(0)
    piece(1, 0)
    piece(3, 0)
    y_step(2)
    product(3, 0)
    product(3, 1)
    x_near(3)
    product(4, 0)
    product(4, 1)
    reduce_y(3)
    x_near(1)
    piece(2, 0)
    piece(0, 3)
    piece(0, 1)
    reduce_y(4)
    product(5, 0)
    product(5, 1)
    x_far(3)
    x_far(1)
    product(6, 0)
    product(6, 1)
    piece(1, 3)
    piece(3, 3)
    piece(1, 1)
    piece(3, 1)
    x_near(2)
    reduce_y(5)
    piece(0, 2)
    piece(2, 3)
    piece(2, 1)
    x_far(2)
    reduce_y(6)
    piece(1, 2)
    piece(3, 2)
    piece(2, 2)

    def finish(t, _):
        rows = pl.ds(pl.multiple_of(t * 64, 64), 64)
        a = acc[rows, :]
        prj[rows, :] = (a * FACTOR).astype(BF)
        dots = jnp.sum(a * cot_v[rows, :].astype(F32), axis=-1, keepdims=True)
        mrow[rows, :] = jnp.broadcast_to(dots * (FACTOR / D), (64, 128))
        return 0

    lax.fori_loop(0, 8, finish, 0)
    for m in range(5):
        reduce_z(m)

    for cp in started:
        cp.wait_send()


def finish_kernel(act_v, back, prj, wgo, inv_v, mrow, gain, pn, mn, proj_o, ig_o, wg_o, pn_o, mn_o, grad, sem):
    copies = [
        pltpu.make_async_copy(prj, proj_o, sem.at[8]),
        pltpu.make_async_copy(wgo, wg_o.at[0], sem.at[9]),
        pltpu.make_async_copy(pn, pn_o, sem.at[10]),
        pltpu.make_async_copy(mn, mn_o, sem.at[11]),
    ]
    for cp in copies:
        cp.start()
    gain_scaled = gain[...].astype(F32).reshape(1, D) * FACTOR

    def grad_in(t, _):
        rows = pl.ds(pl.multiple_of(t * 64, 64), 64)
        inverse = inv_v[rows, :]
        m = mrow[rows, :] * inverse * inverse
        for j in range(32):
            cols = slice(j * 128, (j + 1) * 128)
            a = act_v[rows, cols].astype(F32)
            out = back[j, rows, :] * gain_scaled[:, cols] * inverse - a * m
            grad[rows, cols] = out.astype(BF)
        pltpu.make_async_copy(grad.at[rows], ig_o.at[rows], sem.at[t]).start()
        return 0

    lax.fori_loop(0, 8, grad_in, 0)
    for t in range(8):
        rows = slice(t * 64, (t + 1) * 64)
        pltpu.make_async_copy(grad.at[rows], ig_o.at[rows], sem.at[t]).wait()
    for cp in copies:
        cp.wait()


def shards(fp8_codes, block_scales, outer_params, outer_momentum, activations, norm_gain, cotangent):
    anywhere = pl.BlockSpec(memory_space=pl.ANY)
    vmem = pl.BlockSpec(memory_space=pltpu.VMEM)
    dma = pltpu.SemaphoreType.DMA
    gain_row = norm_gain
    act_v, back, prj, wgo, inv_v, mrow, pn, mn = pl.pallas_call(
        kernel,
        name="exchange",
        out_shape=(
            pltpu.VMEM((T, D), BF),
            pltpu.VMEM((32, T, 128), F32),
            pltpu.VMEM((T, K), BF),
            pltpu.VMEM((T, K), BF),
            pltpu.VMEM((T, 128), F32),
            pltpu.VMEM((T, 128), F32),
            pltpu.VMEM((16, K), F32),
            pltpu.VMEM((16, K), F32),
        ),
        in_specs=[anywhere, vmem, vmem, vmem, anywhere, vmem, anywhere],
        out_specs=(vmem,) * 8,
        scratch_shapes=[
            pltpu.VMEM((512, K), jnp.int32),
            pltpu.VMEM((T, K), BF),
            pltpu.VMEM((32, T, 128), BF),
            pltpu.VMEM((2, 16, 16, K), BF),
            pltpu.VMEM((16, 16, K), BF),
            pltpu.VMEM((16, 16, K), BF),
            pltpu.VMEM((3, 4, 16, K), BF),
            pltpu.VMEM((4, 16, K), BF),
            pltpu.VMEM((3, 16, K), BF),
            pltpu.VMEM((4, 2, 4, 4, 2, 16, K), BF),
            pltpu.VMEM((T, K), F32),
            pltpu.VMEM((T, K), BF),
            pltpu.VMEM((2, 8, T, 128), BF),
            pltpu.VMEM((1024, K), BF),
            pltpu.VMEM((1024, K), F32),
            pltpu.VMEM((1024, K), BF),
            pltpu.VMEM((512, K), BF),
            pltpu.VMEM((512, K), BF),
            dma((3,)),
            dma((2,)),
            dma((7, 2)),
            dma((7,)),
            dma((5,)),
            dma,
            dma((3,)),
            dma((3,)),
            dma((7,)),
            dma((4, 2)),
            dma((4, 4, 2)),
            dma((4, 4)),
            dma((2,)),
            dma((7, 2)),
            dma((7,)),
            dma((5,)),
            dma,
            dma((3,)),
            dma((3,)),
            dma((7,)),
            dma((4,)),
            dma((4, 4)),
            dma((4, 4)),
        ],
        compiler_params=pltpu.CompilerParams(
            collective_id=0, has_side_effects=True, vmem_limit_bytes=45 * 1024 * 1024
        ),
        cost_estimate=pl.CostEstimate(flops=13 * 10**9, bytes_accessed=14 * 2**20, transcendentals=0),
    )(
        fp8_codes, block_scales, outer_params, outer_momentum, activations,
        gain_row, cotangent,
    )
    return pl.pallas_call(
        finish_kernel,
        name="finish",
        out_shape=(
            jax.ShapeDtypeStruct((T, K), BF),
            jax.ShapeDtypeStruct((T, D), BF),
            jax.ShapeDtypeStruct((1, T, K), BF),
            jax.ShapeDtypeStruct((16, K), F32),
            jax.ShapeDtypeStruct((16, K), F32),
        ),
        in_specs=[vmem] * 9,
        out_specs=(anywhere,) * 5,
        scratch_shapes=[pltpu.VMEM((T, D), BF), dma((12,))],
        compiler_params=pltpu.CompilerParams(vmem_limit_bytes=16 * 1024 * 1024),
    )(act_v, back, prj, wgo, inv_v, mrow, gain_row, pn, mn)


def solution(mesh):
    in_specs = (
        P("replica", "fsdp", None),
        P("replica", None, "fsdp"),
        P(("fsdp", "replica"), None),
        P(("fsdp", "replica"), None),
        P(("replica", "fsdp"), None),
        P(),
        P(("replica", "fsdp"), None),
    )
    out_specs = (
        P(("replica", "fsdp"), None),
        P(("replica", "fsdp"), None),
        P("replica", "fsdp", None),
        P(("fsdp", "replica"), None),
        P(("fsdp", "replica"), None),
    )
    return jax.shard_map(shards, mesh=mesh, in_specs=in_specs, out_specs=out_specs, check_vma=False)
```

```python
import functools

import jax
import jax.numpy as jnp
from jax import lax
from jax.experimental import pallas as pl
from jax.experimental.pallas import tpu as pltpu
from jax.sharding import PartitionSpec as P

outer_rate = 0.7
outer_beta = 0.9
epsilon = 1e-05
BF = jnp.bfloat16
F32 = jnp.float32
MESH = pl.DeviceIdType.MESH
D = 4096
T = 512
K = 1024
FACTOR = D ** (-0.5)


def device(x, y, z, c):
    return ((x * 4 + lax.rem(z, 4)) * 2 + c, y * 2 + lax.div(z, 4))


def kernel(
    codes, scales, params, moment, act, gain, cot,
    act_v, back, prj, wgo, inv_v, mrow, pn_o, mn_o,
    codes_v, cot_v, nrm, dec, g1r, g1s, g2r, g2s, g3r, wfull, acc,
    rb, ra, ps, own, pr, zs, zr, grow,
    lsem, bsem, asem, psem, zsem, gsem, g2sem, g3sem, zgsem, ygsem, xgsem, sbsem,
    bss, ass, pss, zss, gss, g2ss, g3ss, zgs, ygs, xgs, sbs,
):
    r = lax.axis_index("replica")
    f = lax.axis_index("fsdp")
    x, zl, c = lax.div(r, 8), lax.rem(lax.div(r, 2), 4), lax.rem(r, 2)
    y, zh = lax.div(f, 2), lax.rem(f, 2)
    z = zh * 4 + zl
    other = 1 - c
    swap = y + 1 - 2 * lax.rem(y, 2)
    p1 = c * (3 - y) + other * swap
    p2 = c * swap + other * (3 - y)
    q = lax.rem(y + 2, 4)
    sibling = device(x, y, z, other)
    dev_p1, dev_p2 = device(x, p1, z, c), device(x, p2, z, c)
    xp = [lax.rem(x + d, 4) for d in (1, 2, 3)]
    zlp = [lax.rem(zl + d, 4) for d in (1, 2, 3)]
    yp = [lax.rem(y + d, 4) for d in (1, 2, 3)]
    zp = [lax.rem(z + d, 8) for d in range(1, 8)]
    dev_x = [device(v, y, z, c) for v in xp]
    dev_zl = [device(x, y, zh * 4 + v, c) for v in zlp]
    dev_y = [device(x, v, z, c) for v in yp]
    dev_z = [device(x, y, v, c) for v in zp]
    dev_z4 = dev_z[3]

    started = []

    def send(src, dst, ss, rs, to):
        cp = pltpu.make_async_remote_copy(
            src_ref=src, dst_ref=dst, send_sem=ss, recv_sem=rs, device_id=to, device_id_type=MESH
        )
        cp.start()
        started.append(cp)

    def arrived(dst, rs):
        pltpu.make_async_remote_copy(
            src_ref=dst, dst_ref=dst, send_sem=bss.at[0], recv_sem=rs, device_id=sibling, device_id_type=MESH
        ).wait_recv()

    load_codes = pltpu.make_async_copy(codes.at[0], codes_v, lsem.at[0])
    load_act = pltpu.make_async_copy(act, act_v, lsem.at[1])
    load_cot = pltpu.make_async_copy(cot, cot_v, lsem.at[2])
    load_codes.start()
    load_act.start()
    load_cot.start()

    barrier = pltpu.get_barrier_semaphore()
    friends = [sibling, *dev_x, *dev_y, *dev_z]
    for to in friends:
        pl.semaphore_signal(barrier, inc=1, device_id=to, device_id_type=MESH)
    pl.semaphore_wait(barrier, len(friends))

    def send_b(k):
        cols = slice(k * 512, (k + 1) * 512)
        send(cot.at[:, cols], rb.at[:, cols], bss.at[k], bsem.at[k], dev_p1)

    send_b(0)

    factors = jnp.exp2((scales[0] - 127).astype(F32)).astype(BF)
    spread = (
        lax.broadcasted_iota(jnp.int32, (8, K), 1) // 128 == lax.broadcasted_iota(jnp.int32, (8, K), 0)
    ).astype(F32).astype(BF)
    acc[...] = lax.dot_general(factors, spread, (((0,), (0,)), ((), ())), preferred_element_type=F32)
    load_codes.wait()

    def decode_half(which):
        def step(g, _):
            rows = pl.ds(pl.multiple_of(g * 32 + which * 16, 16), 16)
            code = codes_v[rows, :]
            field = (code >> 3) & 15
            low = code & 7
            whole = jnp.where(field > 0, low + 8, low * 2) << field
            value = whole.astype(F32) * (acc[rows, :] * (2.0**-10))
            dec[which, g] = jnp.where(code >= 128, -value, value).astype(BF)
            return 0

        lax.fori_loop(0, 16, step, 0)

    decode_half(other)
    send(dec.at[other], g1r, gss, gsem, sibling)
    decode_half(c)
    arrived(g1r, gsem)

    def sum_one(g, _):
        g1s[g] = (dec[c, g].astype(F32) + g1r[g].astype(F32)).astype(BF)
        return 0

    lax.fori_loop(0, 16, sum_one, 0)
    for i in range(3):
        send(g1s.at[pl.ds(xp[i] * 4, 4)], g2r.at[i], g2ss.at[i], g2sem.at[i], dev_x[i])

    load_act.wait()
    gain_row = gain[...].astype(F32).reshape(1, D)
    for j in range(32):
        grow[j] = jnp.broadcast_to(gain_row[:, j * 128 : (j + 1) * 128] * FACTOR, (8, 128))

    def norm(t, _):
        rows = pl.ds(pl.multiple_of(t * 32, 32), 32)
        total = jnp.zeros((32, 128), F32)
        for j in range(32):
            a = act_v[rows, j * 128 : (j + 1) * 128].astype(F32)
            total = total + a * a
        inverse = lax.rsqrt(jnp.sum(total, axis=-1, keepdims=True) / D + epsilon)
        wide = jnp.broadcast_to(inverse, (32, 128))
        inv_v[rows, :] = wide
        for j in range(32):
            a = act_v[rows, j * 128 : (j + 1) * 128].astype(F32)
            nrm[j, rows, :] = (a * wide * gain_row[:, j * 128 : (j + 1) * 128]).astype(BF)
        return 0

    lax.fori_loop(0, 16, norm, 0)
    load_cot.wait()

    halves = (1 - zh, zh)
    left, right, whole = slice(0, 512), slice(512, K), slice(0, K)
    chunks = (
        (0, 0, 1, left), (0, 1, 1, left), (0, 2, 2, left), (0, 0, 2, right), (0, 2, 2, right),
        (1, 0, 2, whole), (1, 2, 2, whole),
    )

    def send_a(m, t):
        i, first, count, _ = chunks[m]
        src = nrm.at[pl.ds((q, p1)[t] * 8 + halves[i] * 4 + first, count)]
        dst = ra.at[t, i * 4 + first : i * 4 + first + count]
        send(src, dst, ass.at[m, t], asem.at[m, t], dev_p1)

    send_a(0, 0)
    send_a(0, 1)

    def product(m, t):
        i, first, count, cols = chunks[m]
        low = i * 4 + first
        if m not in (3, 4):
            arrived(ra.at[t, low : low + count], asem.at[m, t])
        if m < 2:
            send_a(m + 1, t)
        if m == 3 and t == 0:
            arrived(rb.at[:, right], bsem.at[1])
        if m == 4:
            send_a(6, t)
        j = (p2, y)[t] * 8 + halves[i] * 4 + first
        mine = jnp.concatenate([nrm[j + b] for b in range(count)], axis=1)
        theirs = jnp.concatenate([ra[t, low + b] for b in range(count)], axis=1)
        dims = (((0,), (0,)), ((), ()))
        total = lax.dot_general(mine, cot_v[:, cols], dims, preferred_element_type=F32)
        total = total + lax.dot_general(theirs, rb[:, cols], dims, preferred_element_type=F32)
        total = total * FACTOR
        rows = slice(low * 128, (low + count) * 128)
        if t == 0:
            ps[rows, cols] = total.astype(BF)
            send(ps.at[rows, cols], pr.at[rows, cols], pss.at[m], psem.at[m], dev_p2)
        else:
            own[rows, cols] = total

    def reduce_y(m):
        i, first, count, cols = chunks[m]
        rows = slice((i * 4 + first) * 128, (i * 4 + first + count) * 128)
        arrived(pr.at[rows, cols], psem.at[m])
        total = own[rows, cols] + pr[rows, cols].astype(F32)
        if i == 0:
            zs[rows, cols] = total.astype(BF)
            send(zs.at[rows, cols], zr.at[rows, cols], zss.at[m], zsem.at[m], dev_z4)
        else:
            own[rows, cols] = total

    def reduce_z(m):
        _, first, count, cols = chunks[m]
        rows = slice(first * 128, (first + count) * 128)
        arrived(zr.at[rows, cols], zsem.at[m])
        summed = own[512 + first * 128 : 512 + (first + count) * 128, cols]
        wgo[rows, cols] = (summed + zr[rows, cols].astype(F32)).astype(BF)

    def grad_x():
        for i in range(3):
            arrived(g2r.at[i], g2sem.at[i])
        total = g1s[pl.ds(x * 4, 4)].astype(F32)
        for i in range(3):
            total = total + g2r[i].astype(F32)
        g2s[...] = total.astype(BF)
        for i in range(3):
            send(g2s.at[zlp[i]], g3r.at[i], g3ss.at[i], g3sem.at[i], dev_zl[i])

    def grad_z():
        for i in range(3):
            arrived(g3r.at[i], g3sem.at[i])
        total = g2s[zl].astype(F32)
        for i in range(3):
            total = total + g3r[i].astype(F32)
        delta = total / 32.0
        momentum_next = outer_beta * moment[...] + delta
        params_next = params[...] - outer_rate * (delta + outer_beta * momentum_next)
        mn_o[...] = momentum_next
        pn_o[...] = params_next
        wfull[y, zh, x, zl, c] = params_next.astype(BF)
        mine = wfull.at[y, zh, x, zl, c]
        for i in range(7):
            send(mine, mine, zgs.at[i], zgsem.at[i], dev_z[i])

    def gather_z():
        for i in range(7):
            v = lax.rem(z + 7 - i, 8)
            arrived(wfull.at[y, lax.div(v, 4), x, lax.rem(v, 4), c], zgsem.at[i])

    def wblock(vx, vy, core):
        return wfull.at[vy, :, vx, :, core]

    def whalf(vx, vy, half):
        return wfull.at[vy, half, vx, :, c]

    def row_of(d):
        return lax.rem(y + d, 4)

    def y_step(d):
        vy = row_of(d)
        ref = wblock(x, vy, c)
        if d == 0:
            send(ref, ref, ygs.at[0], ygsem.at[vy, 0], dev_y[0])
            send(ref, ref, ygs.at[1], ygsem.at[vy, 0], dev_y[2])
        elif d == 3:
            arrived(ref, ygsem.at[vy, 0])
            send(whalf(x, vy, 0), whalf(x, vy, 0), ygs.at[2], ygsem.at[vy, 0], dev_y[0])
        elif d == 1:
            arrived(ref, ygsem.at[vy, 0])
            send(whalf(x, vy, 1), whalf(x, vy, 1), ygs.at[3], ygsem.at[vy, 1], dev_y[2])
        else:
            arrived(whalf(x, vy, 0), ygsem.at[vy, 0])
            arrived(whalf(x, vy, 1), ygsem.at[vy, 1])
        send(ref, ref, xgs.at[vy, 0], xgsem.at[x, vy, 0], dev_x[0])
        send(ref, ref, xgs.at[vy, 1], xgsem.at[x, vy, 0], dev_x[2])
        send(ref, ref, sbs.at[x, vy], sbsem.at[x, vy], sibling)

    def x_near(d):
        vy = row_of(d)
        for dx, half, to in ((3, 0, 0), (1, 1, 2)):
            vx = xp[dx - 1]
            ref = wblock(vx, vy, c)
            arrived(ref, xgsem.at[vx, vy, 0])
            part = whalf(vx, vy, half)
            send(part, part, xgs.at[vy, 2 + half], xgsem.at[vx, vy, half], dev_x[to])
            send(ref, ref, sbs.at[vx, vy], sbsem.at[vx, vy], sibling)

    def x_far(d):
        vy = row_of(d)
        vx = xp[1]
        for half in range(2):
            arrived(whalf(vx, vy, half), xgsem.at[vx, vy, half])
        ref = wblock(vx, vy, c)
        send(ref, ref, sbs.at[vx, vy], sbsem.at[vx, vy], sibling)

    def piece(dx, dy, first=False):
        vx, vy = lax.rem(x + dx, 4), row_of(dy)
        arrived(wblock(vx, vy, other), sbsem.at[vx, vy])
        w = wfull[vy, :, vx].reshape(256, K)
        j = vy * 8 + vx
        lhs = jnp.concatenate([nrm[j], nrm[j + 4]], axis=1)
        part = jnp.dot(lhs, w, preferred_element_type=F32)
        acc[...] = part if first else acc[...] + part
        b = lax.dot_general(cot_v[...], w, (((1,), (1,)), ((), ())), preferred_element_type=F32)
        for i in range(2):
            scaled = b[:, i * 128 : (i + 1) * 128] * grow[j + 4 * i][0:1, :]
            back[j + 4 * i] = scaled * inv_v[...]

    arrived(rb.at[:, left], bsem.at[0])
    product(0, 0)
    grad_x()
    product(0, 1)
    product(1, 0)
    product(1, 1)
    grad_z()
    product(2, 0)
    product(2, 1)
    gather_z()
    y_step(0)
    reduce_y(0)
    reduce_y(1)
    reduce_y(2)
    piece(0, 0, True)
    x_near(0)
    y_step(3)
    y_step(1)
    send_b(1)
    send_a(5, 0)
    send_a(5, 1)
    x_far(0)
    piece(1, 0)
    piece(3, 0)
    y_step(2)
    product(3, 0)
    product(3, 1)
    x_near(3)
    product(4, 0)
    product(4, 1)
    reduce_y(3)
    x_near(1)
    piece(2, 0)
    piece(0, 3)
    piece(0, 1)
    reduce_y(4)
    product(5, 0)
    product(5, 1)
    x_far(3)
    x_far(1)
    product(6, 0)
    product(6, 1)
    piece(1, 3)
    piece(3, 3)
    piece(1, 1)
    piece(3, 1)
    x_near(2)
    reduce_y(5)
    reduce_z(0)
    reduce_z(1)
    piece(0, 2)
    piece(2, 3)
    piece(2, 1)
    x_far(2)
    reduce_y(6)
    reduce_z(2)
    piece(1, 2)
    piece(3, 2)
    piece(2, 2)

    def finish(t, _):
        rows = pl.ds(pl.multiple_of(t * 64, 64), 64)
        a = acc[rows, :]
        prj[rows, :] = (a * FACTOR).astype(BF)
        dots = jnp.sum(a * cot_v[rows, :].astype(F32), axis=-1, keepdims=True)
        mrow[rows, :] = jnp.broadcast_to(dots * (FACTOR / D), (64, 128))
        return 0

    lax.fori_loop(0, 8, finish, 0)
    for m in (3, 4):
        reduce_z(m)

    for cp in started:
        cp.wait_send()


def finish_kernel(act_v, back, prj, wgo, inv_v, mrow, pn, mn, proj_o, ig_o, wg_o, pn_o, mn_o, grad, sem):
    copies = [
        pltpu.make_async_copy(prj, proj_o, sem.at[8]),
        pltpu.make_async_copy(wgo, wg_o.at[0], sem.at[9]),
        pltpu.make_async_copy(pn, pn_o, sem.at[10]),
        pltpu.make_async_copy(mn, mn_o, sem.at[11]),
    ]
    for cp in copies:
        cp.start()
    def grad_in(t, _):
        rows = pl.ds(pl.multiple_of(t * 64, 64), 64)
        inverse = inv_v[rows, :]
        m = mrow[rows, :] * inverse * inverse
        for j in range(32):
            cols = slice(j * 128, (j + 1) * 128)
            a = act_v[rows, cols].astype(F32)
            out = back[j, rows, :] - a * m
            grad[rows, cols] = out.astype(BF)
        pltpu.make_async_copy(grad.at[rows], ig_o.at[rows], sem.at[t]).start()
        return 0

    lax.fori_loop(0, 8, grad_in, 0)
    for t in range(8):
        rows = slice(t * 64, (t + 1) * 64)
        pltpu.make_async_copy(grad.at[rows], ig_o.at[rows], sem.at[t]).wait()
    for cp in copies:
        cp.wait()


def shards(fp8_codes, block_scales, outer_params, outer_momentum, activations, norm_gain, cotangent):
    anywhere = pl.BlockSpec(memory_space=pl.ANY)
    vmem = pl.BlockSpec(memory_space=pltpu.VMEM)
    dma = pltpu.SemaphoreType.DMA
    gain_row = norm_gain
    act_v, back, prj, wgo, inv_v, mrow, pn, mn = pl.pallas_call(
        kernel,
        name="exchange",
        out_shape=(
            pltpu.VMEM((T, D), BF),
            pltpu.VMEM((32, T, 128), F32),
            pltpu.VMEM((T, K), BF),
            pltpu.VMEM((T, K), BF),
            pltpu.VMEM((T, 128), F32),
            pltpu.VMEM((T, 128), F32),
            pltpu.VMEM((16, K), F32),
            pltpu.VMEM((16, K), F32),
        ),
        in_specs=[anywhere, vmem, vmem, vmem, anywhere, vmem, anywhere],
        out_specs=(vmem,) * 8,
        scratch_shapes=[
            pltpu.VMEM((512, K), jnp.int32),
            pltpu.VMEM((T, K), BF),
            pltpu.VMEM((32, T, 128), BF),
            pltpu.VMEM((2, 16, 16, K), BF),
            pltpu.VMEM((16, 16, K), BF),
            pltpu.VMEM((16, 16, K), BF),
            pltpu.VMEM((3, 4, 16, K), BF),
            pltpu.VMEM((4, 16, K), BF),
            pltpu.VMEM((3, 16, K), BF),
            pltpu.VMEM((4, 2, 4, 4, 2, 16, K), BF),
            pltpu.VMEM((T, K), F32),
            pltpu.VMEM((T, K), BF),
            pltpu.VMEM((2, 8, T, 128), BF),
            pltpu.VMEM((1024, K), BF),
            pltpu.VMEM((1024, K), F32),
            pltpu.VMEM((1024, K), BF),
            pltpu.VMEM((512, K), BF),
            pltpu.VMEM((512, K), BF),
            pltpu.VMEM((32, 8, 128), F32),
            dma((3,)),
            dma((2,)),
            dma((7, 2)),
            dma((7,)),
            dma((5,)),
            dma,
            dma((3,)),
            dma((3,)),
            dma((7,)),
            dma((4, 2)),
            dma((4, 4, 2)),
            dma((4, 4)),
            dma((2,)),
            dma((7, 2)),
            dma((7,)),
            dma((5,)),
            dma,
            dma((3,)),
            dma((3,)),
            dma((7,)),
            dma((4,)),
            dma((4, 4)),
            dma((4, 4)),
        ],
        compiler_params=pltpu.CompilerParams(
            collective_id=0, has_side_effects=True, vmem_limit_bytes=45 * 1024 * 1024
        ),
        cost_estimate=pl.CostEstimate(flops=13 * 10**9, bytes_accessed=14 * 2**20, transcendentals=0),
    )(
        fp8_codes, block_scales, outer_params, outer_momentum, activations,
        gain_row, cotangent,
    )
    return pl.pallas_call(
        finish_kernel,
        name="finish",
        out_shape=(
            jax.ShapeDtypeStruct((T, K), BF),
            jax.ShapeDtypeStruct((T, D), BF),
            jax.ShapeDtypeStruct((1, T, K), BF),
            jax.ShapeDtypeStruct((16, K), F32),
            jax.ShapeDtypeStruct((16, K), F32),
        ),
        in_specs=[vmem] * 8,
        out_specs=(anywhere,) * 5,
        scratch_shapes=[pltpu.VMEM((T, D), BF), dma((12,))],
        compiler_params=pltpu.CompilerParams(vmem_limit_bytes=16 * 1024 * 1024),
    )(act_v, back, prj, wgo, inv_v, mrow, pn, mn)


def solution(mesh):
    in_specs = (
        P("replica", "fsdp", None),
        P("replica", None, "fsdp"),
        P(("fsdp", "replica"), None),
        P(("fsdp", "replica"), None),
        P(("replica", "fsdp"), None),
        P(),
        P(("replica", "fsdp"), None),
    )
    out_specs = (
        P(("replica", "fsdp"), None),
        P(("replica", "fsdp"), None),
        P("replica", "fsdp", None),
        P(("fsdp", "replica"), None),
        P(("fsdp", "replica"), None),
    )
    return jax.shard_map(shards, mesh=mesh, in_specs=in_specs, out_specs=out_specs, check_vma=False)
```
